32 devices in a mesh: section: 4 (over y, x), dp: 8 (over z, core).
Axes of the slice: x: 2, y: 2, z: 4, core: 2. Of those that a mesh axis runs over, the one named last changes fastest.
Arguments:
- images: bfloat16 [16, 16, 16, 768], P('dp'), may hold values from -6 to 6
- roster: int32 [8, 2], P('dp'), may hold values from 0 to 1, each once within a row
- cotangent: bfloat16 [16, 16, 16, 768], P('dp'), may hold values from -6 to 6
- depth_kernel: bfloat16 [4, 7, 7, 768], P('section'), may hold values from -0.875 to 0.875
- up_weight: bfloat16 [4, 768, 3072], P('section'), may hold values from -0.21875 to 0.21875
- down_weight: bfloat16 [4, 3072, 768], P('section'), may hold values from -0.109375 to 0.109375
- layer_scale: float32 [4, 768], P('section'), may hold values from 0.3 to 1
- master: float32 [4, 55752, 128], P('section', 'dp'), may hold values from -0.75 to 0.75
- first_moment: float32 [4, 55752, 128], P('section', 'dp'), may hold values from -6 to 6
- second_moment: float32 [4, 55752, 128], P('section', 'dp'), may hold values from 0.05 to 5
- bucket_bounds: int32 [4, 25], P('section'), may hold values from 0 to 37168, as said below
- bucket_owner: int32 [4, 24], P('section'), may hold values from 0 to 7, as said below
Outputs:
- section_outputs: bfloat16 [4, 16, 16, 16, 768], P('section', 'dp')
- new_master: float32 [4, 55752, 128], P('section', 'dp')
- new_first_moment: float32 [4, 55752, 128], P('section', 'dp')
- new_second_moment: float32 [4, 55752, 128], P('section', 'dp')
The draws below stay inside these ranges and needn't reach their ends.
Inputs may be any that keep to these rules, and one draw needn't show every extreme that they name: `roster`: each row names every slot once. `bucket_bounds`: in each block's row the bounds never fall, the first is 0 and the last is 37168. `bucket_owner`: in each block every owner is named by 3 buckets; the buckets of one owner hold at most 6969 rows together, and some owner holds exactly 6969.
All inputs are finite; a program needn't handle non-finite values.
Results may differ from the reference program's by a relative error of at most 0.028.
Values may be sent and summed in bfloat16 or wider, within the bound.
A program may use at most 128 MiB of HBM per device.

```python
import math
import jax
import jax.numpy as jnp
from jax import lax

C = 768
HID = 3072
KS = 7
H = 16
W = 16
MICRO = 2
GRAN = 128
BPO = 3
SECTIONS = 4
REPLICAS = 8
IMAGES = 16
NROWS = 37164
AVG = 4646
UNITS = 37168
SPREAD = 2323
CAPR = 6969
NB = 24


def bucket_plan(key):

    def one_section(section_key):
        subkeys = jax.random.split(section_key, 6)
        pair_count = REPLICAS // 2
        extra_rows = jax.random.randint(subkeys[0], (pair_count,), 0, SPREAD + 1)
        forced = jax.random.randint(subkeys[1], (), 0, pair_count)
        extra_rows = jnp.where(jnp.arange(pair_count) == forced, SPREAD, extra_rows)
        flip_sign = 1 - 2 * jax.random.randint(subkeys[2], (pair_count,), 0, 2)
        owner_loads = jnp.stack([AVG + flip_sign * extra_rows, AVG - flip_sign * extra_rows], axis=1).reshape(-1)
        owner_loads = owner_loads[jax.random.permutation(subkeys[3], REPLICAS)]
        weights = jax.random.randint(subkeys[4], (REPLICAS, BPO), 1, 5)
        running = jnp.cumsum(weights, axis=1)
        cut_points = owner_loads[:, None] * running // running[:, -1:]
        bucket_sizes = cut_points - jnp.concatenate([jnp.zeros((REPLICAS, 1), cut_points.dtype), cut_points[:, :-1]], axis=1)
        bucket_order = jax.random.permutation(subkeys[5], NB)
        flat_sizes = bucket_sizes.reshape(-1)[bucket_order]
        owners = (jnp.arange(NB) // BPO)[bucket_order]
        bounds = jnp.concatenate([jnp.zeros((1,), flat_sizes.dtype), jnp.cumsum(flat_sizes)])
        return (bounds.astype(jnp.int32), owners.astype(jnp.int32))
    return jax.vmap(one_section)(jax.random.split(jax.random.fold_in(key, 7), SECTIONS))


def draw_bucket_bounds(key, part):
    return bucket_plan(key)[0]


def draw_bucket_owner(key, part):
    return bucket_plan(key)[1]


def block_scale(rng, extent, cuts, low, top_value):
    def one(position, parts):
        draws = jax.random.uniform(jax.random.fold_in(jax.random.fold_in(rng, 6), position), (parts,), jnp.float32, low / len(cuts), top_value / len(cuts))
        return jnp.repeat(jnp.exp(draws), extent[position] // parts).reshape((-1,) + (1,) * (len(extent) - position - 1))

    gain = one(*cuts[0])
    for cut in cuts[1:]:
        gain = gain * one(*cut)
    return gain


def gaussian(stream_key, shape, deviation, bound, pieces=(), held_as=jnp.bfloat16):
    array = jax.random.normal(stream_key, shape, jnp.float32) * deviation
    if len(pieces) > 0:
        array = block_scale(stream_key, shape, pieces, -0.22, 0.18) * array
    return jnp.clip(array, min=-bound, max=bound).astype(held_as)


def setup_inputs(seed: int = 0) -> dict:
    splits = jax.random.split(jax.random.key(seed), 13)
    images = gaussian(splits[0], (IMAGES, H, W, C), 1.0, 6.0, ((0, 8),))
    roster = jax.vmap(lambda own: jax.random.permutation(own, MICRO))(jax.random.split(splits[1], REPLICAS)).reshape((REPLICAS, MICRO)).astype(jnp.int32)
    cotangent = gaussian(splits[2], (IMAGES, H, W, C), 1.0, 6.0, ((0, 8),))
    depth_kernel = gaussian(splits[3], (SECTIONS, KS, KS, C), (KS * KS) ** -0.5, 0.875, ((0, 4),))
    up_weight = gaussian(splits[4], (SECTIONS, C, HID), C ** -0.5, 0.21875, ((0, 4),))
    down_weight = gaussian(splits[5], (SECTIONS, HID, C), HID ** -0.5, 0.109375, ((0, 4),))
    layer_scale = jnp.clip(jnp.exp(math.log(1.0) - 1.2039728 * jax.random.uniform(splits[6], (SECTIONS, C), jnp.float32) ** block_scale(splits[6], (SECTIONS, C), ((0, 4),), -0.2, 0.2)), 0.3, 1.0)
    master = gaussian(splits[7], (SECTIONS, REPLICAS * CAPR, GRAN), 0.05, 0.75, ((0, 4), (1, 8)), jnp.float32)
    first_moment = gaussian(splits[8], (SECTIONS, REPLICAS * CAPR, GRAN), 0.5, 6.0, ((0, 4), (1, 8)), jnp.float32)
    second_moment = jnp.clip(jnp.exp(math.log(5.0) - 4.6051702 * jax.random.uniform(splits[9], (SECTIONS, REPLICAS * CAPR, GRAN), jnp.float32) ** block_scale(splits[9], (SECTIONS, REPLICAS * CAPR, GRAN), ((0, 4), (1, 8)), -0.2, 0.2)), 0.05, 5.0)
    bucket_bounds = draw_bucket_bounds(jax.random.fold_in(splits[12], 71), 0)
    bucket_owner = draw_bucket_owner(jax.random.fold_in(splits[12], 71), 0)
    return dict(images=images, roster=roster, cotangent=cotangent, depth_kernel=depth_kernel, up_weight=up_weight, down_weight=down_weight, layer_scale=layer_scale, master=master, first_moment=first_moment, second_moment=second_moment, bucket_bounds=bucket_bounds, bucket_owner=bucket_owner)


beta_one = 0.9
beta_two = 0.95
learn_rate = 0.01
decay_rate = 0.1
adam_eps = 1e-08
norm_eps = 1e-06
first_fix = 1.0 - 0.9 ** 10
second_fix = 1.0 - 0.95 ** 10

def depthwise(inputs, kernel):
    reach = (kernel.shape[0] - 1) // 2
    return lax.conv_general_dilated(inputs, kernel[:, :, None, :], (1, 1), ((reach, reach), (reach, reach)), dimension_numbers=('NHWC', 'HWIO', 'NHWC'), feature_group_count=inputs.shape[-1], preferred_element_type=jnp.float32)

def gelu_slope(values):
    cumulative = 0.5 * (1.0 + lax.erf(values * 0.7071067811865476))
    return cumulative + values * jnp.exp(-0.5 * values * values) * 0.3989422804014327

def normalize(conv_rows):
    centred = conv_rows - lax.optimization_barrier(jnp.mean(conv_rows, axis=-1, keepdims=True))
    inv_std = lax.rsqrt(lax.optimization_barrier(jnp.mean(centred * centred, axis=-1, keepdims=True)) + norm_eps)
    return (centred * inv_std, inv_std)

def block_forward(block_in, kernel, up_matrix, down_matrix, scale_row):
    channels = block_in.shape[-1]
    conv_rows = depthwise(block_in, kernel).reshape(-1, channels)
    normed_f, inv_std = normalize(conv_rows)
    normed = normed_f.astype(jnp.bfloat16)
    hidden_pre = jnp.dot(normed, up_matrix, preferred_element_type=jnp.float32)
    hidden = jax.nn.gelu(hidden_pre, approximate=False).astype(jnp.bfloat16)
    branch = jnp.dot(hidden, down_matrix, preferred_element_type=jnp.float32)
    block_out = block_in.reshape(-1, channels).astype(jnp.float32) + scale_row * branch
    return (block_out.astype(jnp.bfloat16).reshape(block_in.shape), conv_rows, hidden_pre, branch)

def block_backward(grad_out, block_in, conv_rows, hidden_pre, branch, kernel, up_matrix, down_matrix, scale_row):
    channels = block_in.shape[-1]
    out_rows = grad_out.reshape(-1, channels).astype(jnp.float32)
    scaled = (out_rows * scale_row).astype(jnp.bfloat16)
    scale_terms = out_rows * branch
    hidden = jax.nn.gelu(hidden_pre, approximate=False).astype(jnp.bfloat16)
    grad_hidden = lax.dot_general(scaled, down_matrix, (((1,), (1,)), ((), ())), preferred_element_type=jnp.float32)
    grad_pre = (grad_hidden * gelu_slope(hidden_pre)).astype(jnp.bfloat16)
    normed_f, inv_std = normalize(conv_rows)
    normed = normed_f.astype(jnp.bfloat16)
    grad_normed = lax.dot_general(grad_pre, up_matrix, (((1,), (1,)), ((), ())), preferred_element_type=jnp.float32)
    grad_conv = inv_std * (grad_normed - lax.optimization_barrier(jnp.mean(grad_normed, axis=-1, keepdims=True)) - normed_f * lax.optimization_barrier(jnp.mean(grad_normed * normed_f, axis=-1, keepdims=True)))
    grad_conv = grad_conv.astype(jnp.bfloat16).reshape(block_in.shape)
    back_conv = depthwise(grad_conv, kernel[::-1, ::-1])
    grad_in = (out_rows + back_conv.reshape(-1, channels)).astype(jnp.bfloat16).reshape(block_in.shape)
    return (grad_in, scaled, hidden, grad_pre, normed, grad_conv, scale_terms)

def owner_slots(bounds, owners, owner_id, slot_count, empty_row):
    lengths = bounds[1:] - bounds[:-1]
    mine = (owners == owner_id).astype(jnp.int32)
    taken = lengths * mine
    offsets = jnp.cumsum(taken) - taken
    slot_ids = jnp.arange(slot_count, dtype=jnp.int32)[:, None]
    hits = (mine[None, :] > 0) & (slot_ids >= offsets[None, :]) & (slot_ids < (offsets + lengths)[None, :])
    found = lax.optimization_barrier(jnp.sum(jnp.where(hits, bounds[:-1][None, :] + slot_ids - offsets[None, :], 0), axis=1))
    return jnp.where(jnp.any(hits, axis=1), found, empty_row).astype(jnp.int32)

def kernel_grads(block_in, grad_conv, kernel, replica_count):
    reach = (kernel.shape[0] - 1) // 2
    height, breadth, channels = (block_in.shape[1], block_in.shape[2], block_in.shape[3])
    padded = jnp.pad(block_in.astype(jnp.float32), ((0, 0), (reach, reach), (reach, reach), (0, 0)))
    grad_values = grad_conv.astype(jnp.float32)
    columns = []
    for row_shift in range(2 * reach + 1):
        for col_shift in range(2 * reach + 1):
            window = padded[:, row_shift:row_shift + height, col_shift:col_shift + breadth, :]
            product = (window * grad_values).reshape(replica_count, -1, channels)
            columns.append(lax.optimization_barrier(jnp.sum(product, axis=1)))
    return jnp.stack(columns, axis=1)

def reference(images, roster, cotangent, depth_kernel, up_weight, down_weight, layer_scale, master, first_moment, second_moment, bucket_bounds, bucket_owner):
    picks = (jnp.arange(REPLICAS, dtype=jnp.int32)[:, None] * MICRO + roster).reshape(-1)
    block_in = images[picks]
    inputs = []
    outputs = []
    for section_id in range(SECTIONS):
        inputs.append(block_in)
        block_in = block_forward(block_in, depth_kernel[section_id], up_weight[section_id], down_weight[section_id], layer_scale[section_id])[0]
        outputs.append(block_in)
    section_outputs = jnp.stack(outputs)
    grad_out = cotangent
    per_rows = MICRO * H * W
    masters = []
    firsts = []
    seconds = []
    for section_id in reversed(range(SECTIONS)):
        kernel = depth_kernel[section_id]
        section_in = inputs[section_id]
        forward_parts = block_forward(section_in, kernel, up_weight[section_id], down_weight[section_id], layer_scale[section_id])
        grad_in, scaled, hidden, grad_pre, normed, grad_conv, scale_terms = block_backward(grad_out, section_in, forward_parts[1], forward_parts[2], forward_parts[3], kernel, up_weight[section_id], down_weight[section_id], layer_scale[section_id])
        grad_out = grad_in
        scale_grad = lax.optimization_barrier(jnp.sum(scale_terms.reshape(REPLICAS, per_rows, C), axis=1))
        down_grad = jnp.einsum('rph,rpc->rhc', hidden.astype(jnp.float32).reshape(REPLICAS, per_rows, HID), scaled.astype(jnp.float32).reshape(REPLICAS, per_rows, C))
        up_grad = jnp.einsum('rpc,rph->rch', normed.astype(jnp.float32).reshape(REPLICAS, per_rows, C), grad_pre.astype(jnp.float32).reshape(REPLICAS, per_rows, HID))
        kernel_grad = kernel_grads(section_in, grad_conv, kernel, REPLICAS)
        flat_grad = jnp.concatenate([kernel_grad.reshape(REPLICAS, -1), up_grad.reshape(REPLICAS, -1), down_grad.reshape(REPLICAS, -1), scale_grad], axis=1).astype(jnp.bfloat16)
        flat_grad = lax.optimization_barrier(flat_grad).astype(jnp.float32)
        summed = lax.optimization_barrier(jnp.sum(flat_grad, axis=0)) / REPLICAS
        grad_rows = jnp.concatenate([summed.reshape(NROWS, GRAN), jnp.zeros((UNITS - NROWS + 1, GRAN), summed.dtype)], axis=0)
        slot_rows = jax.vmap(lambda owner_id: owner_slots(bucket_bounds[section_id], bucket_owner[section_id], owner_id, CAPR, UNITS))(jnp.arange(REPLICAS, dtype=jnp.int32)).reshape(-1)
        grad = grad_rows[slot_rows]
        new_first = beta_one * first_moment[section_id] + (1.0 - beta_one) * grad
        new_second = beta_two * second_moment[section_id] + (1.0 - beta_two) * grad * grad
        update = new_first / first_fix / (jnp.sqrt(new_second / second_fix) + adam_eps) + decay_rate * master[section_id]
        masters.append(master[section_id] - learn_rate * update)
        firsts.append(new_first)
        seconds.append(new_second)
    new_master = jnp.stack(masters[::-1])
    new_first_moment = jnp.stack(firsts[::-1])
    new_second_moment = jnp.stack(seconds[::-1])
    return (section_outputs, new_master, new_first_moment, new_second_moment)
```

```python
import functools

import jax
import jax.numpy as jnp
from jax import lax
from jax.experimental import pallas as pl
from jax.experimental.pallas import tpu as pltpu
from jax.sharding import PartitionSpec as P

GRAN = 128


beta_one = 0.9
beta_two = 0.95
learn_rate = 0.01
decay_rate = 0.1
adam_eps = 1e-08
norm_eps = 1e-06
first_fix = 1.0 - 0.9**10
second_fix = 1.0 - 0.95**10


def shifted(block, axis, distance):
    devices = range(lax.axis_size(axis))
    route = [(i - distance, i) for i in devices if i - distance in devices]
    return lax.ppermute(block, axis, route)


def depthwise(inputs, kernel):
    reach = (kernel.shape[0] - 1) // 2
    return lax.conv_general_dilated(
        inputs,
        kernel[:, :, None, :],
        (1, 1),
        ((reach, reach), (reach, reach)),
        dimension_numbers=("NHWC", "HWIO", "NHWC"),
        feature_group_count=inputs.shape[-1],
        preferred_element_type=jnp.float32,
    )


def gelu_slope(values):
    cumulative = 0.5 * (1.0 + lax.erf(values * 0.7071067811865476))
    return cumulative + values * jnp.exp(-0.5 * values * values) * 0.3989422804014327


def normalize(conv_rows):
    centred = conv_rows - jnp.mean(conv_rows, axis=-1, keepdims=True)
    inv_std = lax.rsqrt(jnp.mean(centred * centred, axis=-1, keepdims=True) + norm_eps)
    return (centred * inv_std, inv_std)


def block_forward(block_in, kernel, up_matrix, down_matrix, scale_row):
    channels = block_in.shape[-1]
    conv_rows = depthwise(block_in, kernel).reshape(-1, channels)
    normed_f, inv_std = normalize(conv_rows)
    normed = normed_f.astype(jnp.bfloat16)
    hidden_pre = jnp.dot(normed, up_matrix, preferred_element_type=jnp.float32)
    hidden = jax.nn.gelu(hidden_pre, approximate=False).astype(jnp.bfloat16)
    branch = jnp.dot(hidden, down_matrix, preferred_element_type=jnp.float32)
    block_out = block_in.reshape(-1, channels).astype(jnp.float32) + scale_row * branch
    return (block_out.astype(jnp.bfloat16).reshape(block_in.shape), conv_rows, hidden_pre, branch)


def block_backward(
    grad_out, conv_rows, hidden_pre, kernel, up_matrix, down_matrix, scale_row
):
    channels = grad_out.shape[-1]
    out_rows = grad_out.reshape(-1, channels).astype(jnp.float32)
    scaled = (out_rows * scale_row).astype(jnp.bfloat16)
    grad_hidden = lax.dot_general(
        scaled, down_matrix, (((1,), (1,)), ((), ())), preferred_element_type=jnp.float32
    )
    grad_pre = (grad_hidden * gelu_slope(hidden_pre)).astype(jnp.bfloat16)
    normed_f, inv_std = normalize(conv_rows)
    grad_normed = lax.dot_general(
        grad_pre, up_matrix, (((1,), (1,)), ((), ())), preferred_element_type=jnp.float32
    )
    grad_conv = inv_std * (
        grad_normed
        - jnp.mean(grad_normed, axis=-1, keepdims=True)
        - normed_f * jnp.mean(grad_normed * normed_f, axis=-1, keepdims=True)
    )
    grad_conv = grad_conv.astype(jnp.bfloat16).reshape(grad_out.shape)
    back_conv = depthwise(grad_conv, kernel[::-1, ::-1])
    grad_in = (
        (out_rows + back_conv.reshape(-1, channels)).astype(jnp.bfloat16).reshape(grad_out.shape)
    )
    return (grad_in, grad_pre, grad_conv)


def kernel_grad(block_in, grad_conv, kernel):
    reach = (kernel.shape[0] - 1) // 2
    padded = jnp.pad(block_in, ((reach, reach), (reach, reach), (0, 0)))
    return lax.conv_general_dilated(
        padded[None],
        grad_conv[:, :, None, :],
        (1, 1),
        ((0, 0), (0, 0)),
        dimension_numbers=("NHWC", "HWIO", "NHWC"),
        feature_group_count=block_in.shape[-1],
        preferred_element_type=jnp.float32,
    )[0]


def spread_kernel(step, bounds, owners, *refs):
    *part_refs, spread_ref, rows_ref, gathered = refs
    owner_id = pl.program_id(0)

    @pl.when(owner_id == 0)
    def lay_out():
        base = 0
        for part_ref in part_refs:
            count = part_ref.shape[0]

            def copy(index, carry, part_ref=part_ref, base=base):
                first = pl.multiple_of(index * step, step)
                rows_ref[pl.ds(base + first, step), :] = part_ref[pl.ds(first, step), :]
                return carry

            whole = count // step * step
            lax.fori_loop(0, whole // step, copy, 0)
            if whole < count:
                rows_ref[base + whole : base + count, :] = part_ref[whole:count, :]
            base += count
        rows_ref[base:, :] = jnp.zeros((rows_ref.shape[0] - base, GRAN), jnp.float32)

    def bucket(index, filled):
        start = bounds[index]
        length = jnp.where(owners[index] == owner_id, bounds[index + 1] - start, 0)

        def chunk(part, carry):
            gathered[pl.ds(filled + part * step, step), :] = rows_ref[
                pl.ds(start + part * step, step), :
            ]
            return carry

        lax.fori_loop(0, (length + step - 1) // step, chunk, 0)
        return filled + length

    filled = lax.fori_loop(0, owners.shape[0], bucket, 0)

    def finish(part, carry):
        first = pl.multiple_of(part * 16, 16)
        ids = first + lax.broadcasted_iota(jnp.int32, (16, GRAN), 0)
        kept = jnp.where(ids < filled, gathered[pl.ds(first, 16), :], 0.0)
        spread_ref[0, pl.ds(first, 16), :] = kept.astype(spread_ref.dtype)
        return carry

    lax.fori_loop(0, spread_ref.shape[1] // 16, finish, 0, unroll=4)


def spread_rows(parts, bounds, owners, owner_count, unit_count, slot_rows, step):
    return pl.pallas_call(
        functools.partial(spread_kernel, step),
        out_shape=jax.ShapeDtypeStruct((owner_count, slot_rows, GRAN), jnp.bfloat16),
        grid_spec=pltpu.PrefetchScalarGridSpec(
            num_scalar_prefetch=2,
            grid=(owner_count,),
            in_specs=[pl.BlockSpec(memory_space=pltpu.VMEM)] * len(parts),
            out_specs=pl.BlockSpec((1, slot_rows, GRAN), lambda d, *_: (d, 0, 0)),
            scratch_shapes=[
                pltpu.VMEM((unit_count + step, GRAN), jnp.float32),
                pltpu.VMEM((slot_rows + step, GRAN), jnp.float32),
            ],
        ),
        compiler_params=pltpu.CompilerParams(vmem_limit_bytes=56 * 2**20),
        name="spread_rows",
    )(bounds, owners, *parts)


def adam_kernel(part, count, grad_ref, master_ref, first_ref, second_ref, *outs):
    def chunk(index, carry):
        where = pl.ds(pl.multiple_of(index * part, part), part)
        grad = grad_ref[where, :].astype(jnp.float32) / count
        master = master_ref[where, 0, :]
        new_first = beta_one * first_ref[where, 0, :] + (1.0 - beta_one) * grad
        new_second = beta_two * second_ref[where, 0, :] + (1.0 - beta_two) * grad * grad
        update = (
            new_first / first_fix / (jnp.sqrt(new_second / second_fix) + adam_eps)
            + decay_rate * master
        )
        outs[0][where, 0, :] = master - learn_rate * update
        outs[1][where, 0, :] = new_first
        outs[2][where, 0, :] = new_second
        return carry

    lax.fori_loop(0, grad_ref.shape[0] // part, chunk, 0)


def adam(grad, master, first, second, count):
    block, part = 512, 64
    slots = master.shape[1]
    state = pl.BlockSpec((block, 1, GRAN), lambda i: (i, 0, 0))
    shape = jax.ShapeDtypeStruct((slots, 1, GRAN), jnp.float32)
    results = pl.pallas_call(
        functools.partial(adam_kernel, part, count),
        out_shape=(shape,) * 3,
        grid=(pl.cdiv(slots, block),),
        in_specs=[pl.BlockSpec((block, GRAN), lambda i: (i, 0)), state, state, state],
        out_specs=(state,) * 3,
        name="adam",
    )(grad, *(jnp.swapaxes(held, 0, 1) for held in (master, first, second)))
    return [jnp.swapaxes(held, 0, 1) for held in results]


def pass_forward(activation):
    return shifted(activation, "section", 1)


def pass_backward(gradient):
    return shifted(gradient, "section", -1)


def body(
    images,
    roster,
    cotangent,
    depth_kernel,
    up_weight,
    down_weight,
    layer_scale,
    master,
    first_moment,
    second_moment,
    bucket_bounds,
    bucket_owner,
):
    section_count = lax.axis_size("section")
    replica_count = lax.axis_size("dp")
    section_index = lax.axis_index("section")
    micro_count, height, breadth, channels = images.shape
    kernel = depth_kernel[0]
    up_matrix = up_weight[0]
    down_matrix = down_weight[0]
    scale_row = layer_scale[0]
    hidden_width = up_matrix.shape[1]
    positions = height * breadth
    slot_order = roster[0]
    tick_count = micro_count + section_count - 1

    held_in = jnp.zeros((micro_count + 1, height, breadth, channels), jnp.bfloat16)
    held_conv = jnp.zeros((micro_count + 1, positions, channels), jnp.float32)
    held_pre = jnp.zeros((micro_count + 1, positions, hidden_width), jnp.float32)
    held_branch = jnp.zeros((micro_count + 1, positions, channels), jnp.float32)
    held_out = jnp.zeros((micro_count + 1, height, breadth, channels), jnp.bfloat16)

    def slot_and_place(slot):
        safe_slot = jnp.clip(slot, 0, micro_count - 1)
        return safe_slot, jnp.where(slot == safe_slot, slot, micro_count)

    block_out = None
    for tick in range(tick_count):
        safe_slot, place = slot_and_place(tick - section_index)
        block_in = images[slot_order[safe_slot]]
        if tick > 0:
            block_in = jnp.where(section_index == 0, block_in, pass_forward(block_out))
        block_out, conv_rows, hidden_pre, branch = block_forward(
            block_in[None], kernel, up_matrix, down_matrix, scale_row
        )
        block_out = block_out[0]
        held_in = held_in.at[place].set(block_in)
        held_conv = held_conv.at[place].set(conv_rows)
        held_pre = held_pre.at[place].set(hidden_pre)
        held_branch = held_branch.at[place].set(branch)
        held_out = held_out.at[place].set(block_out)

    slot_in = held_in[:micro_count]
    slot_conv = held_conv[:micro_count]
    slot_pre = held_pre[:micro_count]
    slot_branch = held_branch[:micro_count]
    slot_out = held_out[:micro_count]

    held_grad = jnp.zeros((micro_count + 1, height, breadth, channels), jnp.bfloat16)
    held_grad_pre = jnp.zeros((micro_count + 1, positions, hidden_width), jnp.bfloat16)
    held_grad_conv = jnp.zeros((micro_count + 1, height, breadth, channels), jnp.bfloat16)
    steps_after = section_count - 1 - section_index
    grad_in = None
    for tick in range(tick_count):
        safe_slot, place = slot_and_place(tick - steps_after)
        grad_out = cotangent[safe_slot]
        if tick > 0:
            grad_out = jnp.where(steps_after == 0, grad_out, pass_backward(grad_in))
        grad_in, grad_pre, grad_conv = block_backward(
            grad_out[None],
            slot_conv[safe_slot],
            slot_pre[safe_slot],
            kernel,
            up_matrix,
            down_matrix,
            scale_row,
        )
        grad_in = grad_in[0]
        held_grad = held_grad.at[place].set(grad_out)
        held_grad_pre = held_grad_pre.at[place].set(grad_pre)
        held_grad_conv = held_grad_conv.at[place].set(grad_conv[0])

    out_rows = held_grad[:micro_count].reshape(-1, channels).astype(jnp.float32)
    grad_pre = held_grad_pre[:micro_count].reshape(-1, hidden_width)
    grad_conv = held_grad_conv[:micro_count]
    scaled = (out_rows * scale_row).astype(jnp.bfloat16)
    hidden = jax.nn.gelu(slot_pre.reshape(-1, hidden_width), approximate=False).astype(jnp.bfloat16)
    normed = normalize(slot_conv.reshape(-1, channels))[0].astype(jnp.bfloat16)
    up_sum = lax.dot_general(
        normed, grad_pre, (((0,), (0,)), ((), ())), preferred_element_type=jnp.float32
    )
    down_sum = lax.dot_general(
        hidden, scaled, (((0,), (0,)), ((), ())), preferred_element_type=jnp.float32
    )
    kernel_sum = sum(kernel_grad(slot_in[m], grad_conv[m], kernel) for m in range(micro_count))
    scale_sum = jnp.sum(out_rows * slot_branch.reshape(-1, channels), axis=0)
    parts = [part.reshape(-1, GRAN) for part in (kernel_sum, up_sum, down_sum, scale_sum)]
    row_count = sum(part.shape[0] for part in parts)
    unit_count = -(-row_count // replica_count) * replica_count
    slot_count = master.shape[1]
    step = 128
    slot_rows = -(-slot_count // 16) * 16
    spread = spread_rows(
        parts, bucket_bounds[0], bucket_owner[0], replica_count, unit_count, slot_rows, step
    )
    grad = lax.psum_scatter(
        spread.reshape(-1, GRAN), "dp", scatter_dimension=0, tiled=True
    )
    new_master, new_first, new_second = adam(
        grad, master, first_moment, second_moment, replica_count
    )
    return (slot_out[None], new_master, new_first, new_second)


def solution(mesh):
    placed = (
        P("dp", None, None, None),
        P("dp", None),
        P("dp", None, None, None),
        P("section", None, None, None),
        P("section", None, None),
        P("section", None, None),
        P("section", None),
        P("section", "dp", None),
        P("section", "dp", None),
        P("section", "dp", None),
        P("section", None),
        P("section", None),
    )
    return jax.shard_map(
        body,
        mesh=mesh,
        in_specs=placed,
        out_specs=(
            P("section", "dp", None, None, None),
            P("section", "dp", None),
            P("section", "dp", None),
            P("section", "dp", None),
        ),
        check_vma=False,
    )
```
